32 devices in a mesh: owner: 8 (over y, x, core), view: 4 (over z).
Axes of the slice: x: 2, y: 2, z: 4, core: 2. Of those that a mesh axis runs over, the one named last changes fastest.
Arguments:
- first_view: bfloat16 [1472, 1024], P('owner'), may hold values from -27 to 27
- second_view: bfloat16 [1472, 1024], P(('owner', 'view')), may hold values from -6 to 6
- partner: int32 [1472], P('owner'), may hold values from 0 to 1471, each once
Outputs:
- grad_first: float32 [1472, 1024], P('owner', 'view')
- grad_second: float32 [1472, 1024], P(('owner', 'view'))
The draws below stay inside these ranges and needn't reach their ends.
Inputs may be any that keep to these rules, and one draw needn't show every extreme that they name: partner is a permutation of the batch.
All inputs are finite; a program needn't handle non-finite values.
Results may differ from the reference program's by a relative error of at most 0.0019.
Values may be sent and summed in bfloat16 or wider, within the bound.
A program may use at most 64 MiB of HBM per device.

```python
import math
import jax
import jax.numpy as jnp
from jax import lax

D = 1024
ROWS = 184
N = 1472


def common_embedding(key):
    return jnp.clip(jax.random.normal(key, (N, D), jnp.float32), -6.0, 6.0)


def draw_second_view(key, part):
    shared = common_embedding(key)
    key = jax.random.fold_in(key, 5)
    noise = jax.random.normal(key, (N, D), jnp.float32)
    index = jnp.arange(N, dtype=jnp.int32)
    before = jnp.maximum(index - 1, 0)
    near = jnp.clip(0.99 * shared[before] + 0.1 * noise, -6.0, 6.0)
    chosen = (index % 64 == 1)[:, None]
    return jnp.where(chosen, near, shared).astype(jnp.bfloat16)


def draw_first_view(key, part):
    shared = common_embedding(key)
    key = jax.random.fold_in(key, 7)
    keys = jax.random.split(key, 4)
    base = jnp.clip(jax.random.normal(keys[0], (N, D), jnp.float32), -6.0, 6.0)
    index = jnp.arange(N, dtype=jnp.int32)
    anchor = index - index % 64
    level = jax.random.uniform(keys[3], (N, 1), jnp.float32, 1.2, 2.0)
    factor = jnp.where(index % 64 == 1, 0.992, 1.0).astype(jnp.float32)[:, None]
    size_row = level[anchor] * (100.0 / math.sqrt(D)) * factor
    aligned = size_row * jnp.sign(shared[anchor])
    chosen = (index % 64 < 2)[:, None]
    return jnp.where(chosen, aligned, base).astype(jnp.bfloat16)


def setup_inputs(seed: int = 0) -> dict:
    arg_keys = jax.random.split(jax.random.key(seed), 4)
    return {
        "first_view": draw_first_view(jax.random.fold_in(arg_keys[3], 71), 0),
        "second_view": draw_second_view(jax.random.fold_in(arg_keys[3], 71), 0),
        "partner": jax.random.permutation(arg_keys[2], N).astype(jnp.int32),
    }


def reference(first_view, second_view, partner):
    total = first_view.shape[0]
    logit_scale = 2.0 / math.sqrt(D)
    blocks_first = first_view.reshape(total // ROWS, ROWS, D)
    blocks_partner = partner.reshape(total // ROWS, ROWS)
    column_ids = jnp.arange(total, dtype=jnp.int32)

    def score_block(rows_first):
        return logit_scale * jnp.dot(rows_first, second_view.T, preferred_element_type=jnp.float32)

    def stats_step(totals, rows_first):
        col_peak, col_mass = totals
        scores = score_block(rows_first)
        row_peak = lax.optimization_barrier(jnp.max(scores, axis=1))
        row_lse = row_peak + jnp.log(lax.optimization_barrier(jnp.sum(jnp.exp(scores - row_peak[:, None]), axis=1)))
        new_peak = jnp.maximum(col_peak, lax.optimization_barrier(jnp.max(scores, axis=0)))
        col_mass = col_mass * jnp.exp(col_peak - new_peak) + lax.optimization_barrier(jnp.sum(jnp.exp(scores - new_peak[None, :]), axis=0))
        return ((new_peak, col_mass), row_lse)
    initial = (jnp.full((total,), -jnp.inf, jnp.float32), jnp.zeros((total,), jnp.float32))
    (col_peak, col_mass), row_lse = lax.scan(stats_step, initial, blocks_first)
    col_lse = col_peak + jnp.log(col_mass)

    def grad_step(grad_second, item):
        rows_first, rows_partner, rows_lse = item
        scores = score_block(rows_first)
        target = (rows_partner[:, None] == column_ids[None, :]).astype(jnp.float32)
        weights = (0.5 * (jnp.exp(scores - rows_lse[:, None]) + jnp.exp(scores - col_lse[None, :])) - target).astype(jnp.bfloat16)
        grad_rows = logit_scale * jnp.dot(weights, second_view, preferred_element_type=jnp.float32)
        grad_second = grad_second + logit_scale * jnp.dot(weights.T, rows_first, preferred_element_type=jnp.float32)
        return (grad_second, grad_rows)
    grad_second, grad_blocks = lax.scan(grad_step, jnp.zeros((total, D), jnp.float32), (blocks_first, blocks_partner, row_lse))
    return (grad_blocks.reshape(total, D), grad_second)
```

```python
import functools
import math

import jax
import jax.numpy as jnp
from jax import lax
from jax.experimental import pallas as pl
from jax.experimental.pallas import tpu as pltpu
from jax.sharding import PartitionSpec as P

LOW = -1e30
LANES = 128


def round_up(value, multiple):
    return (value + multiple - 1) // multiple * multiple


def kernel(
    owners, views, shard_rows,
    first_ref, second_ref, partner_ref, g1_ref, g2_ref,
    xs, fz, pbuf, wt, row_msg, col_msg, part1_send, part1_recv, merge_send, merge_recv, own2, part2_send, part2_recv,
    x_send, x_recv, xf_send, row_send, row_recv, col_send, col_recv, p1_send, p1_recv, m_send, m_recv, p2_send, p2_recv,
):
    chips = owners // 2
    rows, features = first_ref.shape
    pad = xs.shape[2]
    half = chips * pad
    columns = 2 * half
    tall = fz.shape[0]
    width = features // views
    scale = 2.0 / math.sqrt(features)
    owner = lax.axis_index("owner")
    view = lax.axis_index("view")
    chip = owner // 2
    core = owner % 2
    other = 1 - core

    def send(src, dst, send_sem, recv_sem, to_owner, to_view):
        return pltpu.make_async_remote_copy(
            src_ref=src, dst_ref=dst, send_sem=send_sem, recv_sem=recv_sem,
            device_id=(to_owner, to_view), device_id_type=pl.DeviceIdType.MESH,
        )

    barrier = pltpu.get_barrier_semaphore()
    for k in range(1, owners):
        pl.semaphore_signal(
            barrier, inc=1, device_id=((owner + k) % owners, view), device_id_type=pl.DeviceIdType.MESH
        )
    for k in range(1, views):
        pl.semaphore_signal(
            barrier, inc=1, device_id=(owner, (view + k) % views), device_id_type=pl.DeviceIdType.MESH
        )
    mine = second_ref[...]
    xs[core, chip] = jnp.concatenate([mine, jnp.zeros((pad - shard_rows, features), mine.dtype)], axis=0)
    pl.semaphore_wait(barrier, owners - 1 + views - 1)

    waits = []

    def block_send(core_of, chip_of, sems, index, to_owner):
        block = xs.at[core_of, chip_of]
        copy = send(block, block, sems.at[index], x_recv.at[core_of, chip_of], to_owner, view)
        copy.start()
        waits.append(copy)

    for k in range(1, chips):
        block_send(core, chip, x_send, k, (chip + k) % chips * 2 + core)
    block_send(core, chip, x_send, 0, chip * 2 + other)

    fz[0:rows, :] = first_ref[...]
    fz[rows:tall, :] = jnp.zeros((tall - rows, features), fz.dtype)
    pbuf[...] = jnp.zeros_like(pbuf)
    pbuf[:, 0:rows] = jnp.broadcast_to(partner_ref[...], (LANES, rows))
    partner = pbuf[...].T[0:rows]

    def block_wait(core_of, chip_of):
        block = xs.at[core_of, chip_of]
        send(block, block, x_send.at[0], x_recv.at[core_of, chip_of], owner, view).wait_recv()

    for k in range(1, chips):
        source = (chip + chips - k) % chips
        block_wait(core, source)
        block_send(core, source, xf_send, k, chip * 2 + other)
    for k in range(chips):
        block_wait(other, (chip + chips - k) % chips)

    position = lax.broadcasted_iota(jnp.int32, (1, columns), 1)
    inner = position % pad
    valid = inner < shard_rows
    slot = position // pad
    column_owner = slot % chips * 2 + slot // chips
    column_ids = jnp.where(valid, (column_owner * views + view) * shard_rows + inner, -1)
    gathered = xs[...].reshape(columns, features)
    scores = scale * lax.dot_general(
        first_ref[...], gathered, (((1,), (1,)), ((), ())), preferred_element_type=jnp.float32
    )
    scores = jnp.where(valid, scores, LOW)
    row_peak = jnp.max(scores, axis=1, keepdims=True)
    row_mass = jnp.sum(jnp.exp(scores - row_peak), axis=1, keepdims=True)
    col_peak = jnp.max(scores, axis=0, keepdims=True)
    col_mass = jnp.sum(jnp.exp(scores - col_peak), axis=0, keepdims=True)
    lane = lax.broadcasted_iota(jnp.int32, (rows, LANES), 1)
    stats = jnp.where(lane == 0, row_peak, row_mass)
    stats = jnp.concatenate([stats, jnp.zeros((tall - rows, LANES), jnp.float32)], axis=0).T
    row_msg[view, :, 0:tall] = stats[0:1]
    row_msg[view, :, tall:] = stats[1:2]
    col_msg[owner, :, 0:columns] = col_peak
    col_msg[owner, :, columns:] = col_mass
    for k in range(1, owners):
        to = (owner + k) % owners
        copy = send(col_msg.at[owner], col_msg.at[owner], col_send.at[k], col_recv.at[owner], to, view)
        copy.start()
        waits.append(copy)
    for k in range(1, views):
        to = (view + k) % views
        copy = send(row_msg.at[view], row_msg.at[view], row_send.at[k], row_recv.at[view], owner, to)
        copy.start()
        waits.append(copy)
    for k in range(1, views):
        source = (view + k) % views
        send(row_msg.at[source], row_msg.at[source], row_send.at[0], row_recv.at[source], owner, view).wait_recv()
    for k in range(1, owners):
        source = (owner + k) % owners
        send(col_msg.at[source], col_msg.at[source], col_send.at[0], col_recv.at[source], owner, view).wait_recv()

    def log_sum(msg, count, length):
        peaks = [msg[k, :, 0:length] for k in range(count)]
        peak = functools.reduce(jnp.maximum, peaks)
        mass = sum(msg[k, :, length:] * jnp.exp(peaks[k] - peak) for k in range(count))
        return peak + jnp.log(mass)

    row_lse = log_sum(row_msg, views, tall)
    col_lse = log_sum(col_msg, owners, columns)
    row_lse = jnp.broadcast_to(row_lse, (LANES, tall)).T[0:rows]
    repeat = columns // LANES
    row_lse = jnp.concatenate([row_lse] * repeat, axis=1)
    target = (jnp.concatenate([partner] * repeat, axis=1) == column_ids).astype(jnp.float32)
    weights = 0.5 * (jnp.exp(scores - row_lse) + jnp.exp(scores - col_lse)) - target

    left = weights.astype(jnp.bfloat16)

    def part1(index):
        start = pl.multiple_of(index * width, LANES)
        right = xs[:, :, :, pl.ds(start, width)].reshape(columns, width)
        return scale * jnp.dot(left, right, preferred_element_type=jnp.float32)

    for k in [2, 1, 3]:
        to = (view + k) % views
        part1_send[k, 0:rows] = part1(to).astype(jnp.bfloat16)
        copy = send(part1_send.at[k], part1_recv.at[k], p1_send.at[k], p1_recv.at[k], owner, to)
        copy.start()
        waits.append(copy)

    wide = jnp.concatenate([weights, jnp.zeros((tall - rows, columns), jnp.float32)], axis=0)
    wt[...] = wide.T.astype(jnp.bfloat16).reshape(2, half, tall)
    merge_send[...] = scale * jnp.dot(wt[other], fz[...], preferred_element_type=jnp.float32)
    merge = send(merge_send, merge_recv, m_send, m_recv, chip * 2 + other, view)
    merge.start()
    waits.append(merge)
    own2[...] = (scale * jnp.dot(wt[core], fz[...], preferred_element_type=jnp.float32))
    own1 = part1(view)
    merge.wait_recv()

    def merged(index):
        start = pl.multiple_of(index * pad, 16)
        return own2[pl.ds(start, pad), :] + merge_recv[pl.ds(start, pad), :]

    for k in range(1, chips):
        to = (chip + k) % chips
        part2_send[k] = merged(to).astype(jnp.bfloat16)
        copy = send(part2_send.at[k], part2_recv.at[k], p2_send.at[k], p2_recv.at[k], to * 2 + core, view)
        copy.start()
        waits.append(copy)
    total2 = merged(chip)
    for k in range(1, chips):
        send(part2_send.at[k], part2_recv.at[k], p2_send.at[k], p2_recv.at[k], owner, view).wait_recv()
        total2 += part2_recv[k].astype(jnp.float32)
    g2_ref[...] = total2[0:shard_rows]
    for k in range(1, views):
        send(part1_send.at[k], part1_recv.at[k], p1_send.at[k], p1_recv.at[k], owner, view).wait_recv()
        own1 += part1_recv[k, 0:rows].astype(jnp.float32)
    g1_ref[...] = own1
    for copy in waits:
        copy.wait_send()


def shards(first_view, second_view, partner):
    owners = lax.axis_size("owner")
    views = lax.axis_size("view")
    chips = owners // 2
    rows, features = first_view.shape
    shard_rows = second_view.shape[0]
    pad = round_up(shard_rows, 16)
    while 2 * chips * pad % LANES:
        pad += 16
    columns = owners * pad
    tall = round_up(rows, LANES)
    deep = round_up(rows, 16)
    width = features // views
    dma = pltpu.SemaphoreType.DMA
    vmem = pl.BlockSpec(memory_space=pltpu.VMEM)
    return pl.pallas_call(
        functools.partial(kernel, owners, views, shard_rows),
        out_shape=(
            jax.ShapeDtypeStruct((rows, width), jnp.float32),
            jax.ShapeDtypeStruct((shard_rows, features), jnp.float32),
        ),
        in_specs=[vmem] * 3,
        out_specs=(vmem, vmem),
        scratch_shapes=[
            pltpu.VMEM((2, chips, pad, features), jnp.bfloat16),
            pltpu.VMEM((tall, features), jnp.bfloat16),
            pltpu.VMEM((LANES, tall), jnp.int32),
            pltpu.VMEM((2, chips * pad, tall), jnp.bfloat16),
            pltpu.VMEM((views, 1, 2 * tall), jnp.float32),
            pltpu.VMEM((owners, 1, 2 * columns), jnp.float32),
            pltpu.VMEM((views, deep, width), jnp.bfloat16),
            pltpu.VMEM((views, deep, width), jnp.bfloat16),
            pltpu.VMEM((chips * pad, features), jnp.float32),
            pltpu.VMEM((chips * pad, features), jnp.float32),
            pltpu.VMEM((chips * pad, features), jnp.float32),
            pltpu.VMEM((chips, pad, features), jnp.bfloat16),
            pltpu.VMEM((chips, pad, features), jnp.bfloat16),
            dma((chips,)),
            dma((2, chips)),
            dma((chips,)),
            dma((views,)),
            dma((views,)),
            dma((owners,)),
            dma((owners,)),
            dma((views,)),
            dma((views,)),
            dma,
            dma,
            dma((chips,)),
            dma((chips,)),
        ],
        compiler_params=pltpu.CompilerParams(
            collective_id=0, has_side_effects=True, vmem_limit_bytes=60 * 1024 * 1024
        ),
    )(first_view, second_view, partner.reshape(1, rows))


def solution(mesh):
    in_specs = (P("owner", None), P(("owner", "view"), None), P("owner"))
    out_specs = (P("owner", "view"), P(("owner", "view"), None))
    return jax.shard_map(shards, mesh=mesh, in_specs=in_specs, out_specs=out_specs, check_vma=False)
```

```python
import functools
import math

import jax
import jax.numpy as jnp
from jax import lax
from jax.experimental import pallas as pl
from jax.experimental.pallas import tpu as pltpu
from jax.sharding import PartitionSpec as P

LOW = -1e30
LANES = 128


def round_up(value, multiple):
    return (value + multiple - 1) // multiple * multiple


def kernel(
    owners, views, shard_rows,
    first_ref, second_ref, partner_ref, g1_ref, g2_ref,
    first_in, second_in, partner_in, xs, fz, pbuf, row_msg, col_msg, part1_send, part1_recv, merge_send, merge_recv, own2, part2_send, part2_recv,
    in_sem, x_send, x_recv, xf_send, row_send, row_recv, col_send, col_recv, p1_send, p1_recv, m_send, m_recv, p2_send, p2_recv,
):
    chips = owners // 2
    rows, features = first_ref.shape
    pad = xs.shape[2]
    half = chips * pad
    tall = fz.shape[0]
    width = features // views
    scale = 2.0 / math.sqrt(features)
    owner = lax.axis_index("owner")
    view = lax.axis_index("view")
    chip = owner // 2
    core = owner % 2
    other = 1 - core

    def send(src, dst, send_sem, recv_sem, to_owner, to_view):
        return pltpu.make_async_remote_copy(
            src_ref=src, dst_ref=dst, send_sem=send_sem, recv_sem=recv_sem,
            device_id=(to_owner, to_view), device_id_type=pl.DeviceIdType.MESH,
        )

    loads = [
        pltpu.make_async_copy(src, dst, in_sem.at[k])
        for k, (src, dst) in enumerate([(second_ref, second_in), (first_ref, first_in), (partner_ref, partner_in)])
    ]
    barrier = pltpu.get_barrier_semaphore()
    for k in range(1, owners):
        pl.semaphore_signal(
            barrier, inc=1, device_id=((owner + k) % owners, view), device_id_type=pl.DeviceIdType.MESH
        )
    for k in range(1, views):
        pl.semaphore_signal(
            barrier, inc=1, device_id=(owner, (view + k) % views), device_id_type=pl.DeviceIdType.MESH
        )
    for load in loads:
        load.start()
    loads[0].wait()
    mine = second_in[...]
    xs[core, chip] = jnp.concatenate([mine, jnp.zeros((pad - shard_rows, features), mine.dtype)], axis=0)
    pl.semaphore_wait(barrier, owners - 1 + views - 1)

    waits = []

    def block_send(core_of, chip_of, sems, index, to_owner):
        block = xs.at[core_of, chip_of]
        copy = send(block, block, sems.at[index], x_recv.at[core_of, chip_of], to_owner, view)
        copy.start()
        waits.append(copy)

    for k in range(1, chips):
        block_send(core, chip, x_send, k, (chip + k) % chips * 2 + core)
    block_send(core, chip, x_send, 0, chip * 2 + other)

    loads[1].wait()
    loads[2].wait()
    fz[0:rows, :] = first_in[...]
    fz[rows:tall, :] = jnp.zeros((tall - rows, features), fz.dtype)
    pbuf[...] = jnp.zeros_like(pbuf)
    pbuf[:, 0:rows] = jnp.broadcast_to(partner_in[...], (LANES, rows))
    copies = round_up(half, LANES) // LANES

    def spread(column):
        return jnp.concatenate([column] * copies, axis=1)[:, 0:half]

    partner = spread(pbuf[...].T[0:rows])
    position = lax.broadcasted_iota(jnp.int32, (1, half), 1)
    inner = position % pad
    slot = position // pad
    valid = inner < shard_rows

    def target_of(core_of):
        ids = ((slot * 2 + core_of) * views + view) * shard_rows + inner
        return (partner == jnp.where(valid, ids, -1)).astype(jnp.float32)

    sides = (core, other)
    targets = [target_of(side) for side in sides]

    def block_wait(core_of, chip_of):
        block = xs.at[core_of, chip_of]
        send(block, block, x_send.at[0], x_recv.at[core_of, chip_of], owner, view).wait_recv()

    def score(side):
        block = xs[side].reshape(half, features)
        values = scale * lax.dot_general(
            first_in[...], block, (((1,), (1,)), ((), ())), preferred_element_type=jnp.float32
        )
        return jnp.where(valid, values, LOW)

    def col_stats(side, values):
        peak = jnp.max(values, axis=0, keepdims=True)
        col_msg[owner, side, :, 0:half] = peak
        col_msg[owner, side, :, half:] = jnp.sum(jnp.exp(values - peak), axis=0, keepdims=True)

    for k in range(1, chips):
        source = (chip + chips - k) % chips
        block_wait(core, source)
        block_send(core, source, xf_send, k, chip * 2 + other)
    scores = [score(core)]
    col_stats(core, scores[0])
    for k in range(chips):
        block_wait(other, (chip + chips - k) % chips)
    scores.append(score(other))
    col_stats(other, scores[1])
    for k in range(1, owners):
        to = (owner + k) % owners
        copy = send(col_msg.at[owner], col_msg.at[owner], col_send.at[k], col_recv.at[owner], to, view)
        copy.start()
        waits.append(copy)
    row_peak = functools.reduce(jnp.maximum, [jnp.max(values, axis=1, keepdims=True) for values in scores])
    row_mass = sum(jnp.sum(jnp.exp(values - row_peak), axis=1, keepdims=True) for values in scores)
    lane = lax.broadcasted_iota(jnp.int32, (rows, LANES), 1)
    stats = jnp.where(lane == 0, row_peak, row_mass)
    stats = jnp.concatenate([stats, jnp.zeros((tall - rows, LANES), jnp.float32)], axis=0).T
    row_msg[view, :, 0:tall] = stats[0:1]
    row_msg[view, :, tall:] = stats[1:2]
    for k in range(1, views):
        to = (view + k) % views
        copy = send(row_msg.at[view], row_msg.at[view], row_send.at[k], row_recv.at[view], owner, to)
        copy.start()
        waits.append(copy)
    for k in range(1, owners):
        source = (owner + k) % owners
        send(col_msg.at[source], col_msg.at[source], col_send.at[0], col_recv.at[source], owner, view).wait_recv()

    def log_sum(parts, length):
        peaks = [part[:, 0:length] for part in parts]
        peak = functools.reduce(jnp.maximum, peaks)
        mass = sum(part[:, length:] * jnp.exp(own - peak) for part, own in zip(parts, peaks))
        return peak + jnp.log(mass)

    by_col = [
        jnp.exp(values - log_sum([col_msg[k, side] for k in range(owners)], half))
        for side, values in zip(sides, scores)
    ]
    for k in range(1, views):
        source = (view + k) % views
        send(row_msg.at[source], row_msg.at[source], row_send.at[0], row_recv.at[source], owner, view).wait_recv()
    row_lse = log_sum([row_msg[k] for k in range(views)], tall)
    row_lse = spread(jnp.broadcast_to(row_lse, (LANES, tall)).T[0:rows])
    weights = [
        0.5 * (jnp.exp(values - row_lse) + by) - target for values, by, target in zip(scores, by_col, targets)
    ]

    left = [values.astype(jnp.bfloat16) for values in weights]

    def part1(index):
        start = pl.multiple_of(index * width, LANES)
        return scale * sum(
            jnp.dot(
                values, xs[side, :, :, pl.ds(start, width)].reshape(half, width),
                preferred_element_type=jnp.float32,
            )
            for side, values in zip(sides, left)
        )

    for k in list(range(2, views)) + [1]:
        to = (view + k) % views
        part1_send[k, 0:rows] = part1(to).astype(jnp.bfloat16)
        copy = send(part1_send.at[k], part1_recv.at[k], p1_send.at[k], p1_recv.at[k], owner, to)
        copy.start()
        waits.append(copy)

    def part2(values):
        tall_values = jnp.concatenate([values, jnp.zeros((tall - rows, half), jnp.float32)], axis=0)
        return scale * jnp.dot(tall_values.T.astype(jnp.bfloat16), fz[...], preferred_element_type=jnp.float32)

    merge_send[...] = part2(weights[1])
    merge = send(merge_send, merge_recv, m_send, m_recv, chip * 2 + other, view)
    merge.start()
    waits.append(merge)
    own2[...] = part2(weights[0])
    own1 = part1(view)
    merge.wait_recv()

    def merged(index):
        start = pl.multiple_of(index * pad, 16)
        return own2[pl.ds(start, pad), :] + merge_recv[pl.ds(start, pad), :]

    for k in range(1, chips):
        to = (chip + k) % chips
        part2_send[k] = merged(to).astype(jnp.bfloat16)
        copy = send(part2_send.at[k], part2_recv.at[k], p2_send.at[k], p2_recv.at[k], to * 2 + core, view)
        copy.start()
        waits.append(copy)
    total2 = merged(chip)
    for k in range(1, chips):
        send(part2_send.at[k], part2_recv.at[k], p2_send.at[k], p2_recv.at[k], owner, view).wait_recv()
        total2 += part2_recv[k].astype(jnp.float32)
    g2_ref[...] = total2[0:shard_rows]
    for k in range(1, views):
        send(part1_send.at[k], part1_recv.at[k], p1_send.at[k], p1_recv.at[k], owner, view).wait_recv()
        own1 += part1_recv[k, 0:rows].astype(jnp.float32)
    g1_ref[...] = own1
    for copy in waits:
        copy.wait_send()


def shards(first_view, second_view, partner):
    owners = lax.axis_size("owner")
    views = lax.axis_size("view")
    chips = owners // 2
    rows, features = first_view.shape
    shard_rows = second_view.shape[0]
    pad = round_up(shard_rows, 16)
    half = chips * pad
    tall = round_up(rows, LANES)
    deep = round_up(rows, 16)
    width = features // views
    dma = pltpu.SemaphoreType.DMA
    vmem = pl.BlockSpec(memory_space=pltpu.VMEM)
    hbm = pl.BlockSpec(memory_space=pl.ANY)
    return pl.pallas_call(
        functools.partial(kernel, owners, views, shard_rows),
        out_shape=(
            pltpu.VMEM((rows, width), jnp.float32),
            pltpu.VMEM((shard_rows, features), jnp.float32),
        ),
        in_specs=[hbm] * 3,
        out_specs=(vmem, vmem),
        scratch_shapes=[
            pltpu.VMEM((rows, features), jnp.bfloat16),
            pltpu.VMEM((shard_rows, features), jnp.bfloat16),
            pltpu.VMEM((1, rows), jnp.int32),
            pltpu.VMEM((2, chips, pad, features), jnp.bfloat16),
            pltpu.VMEM((tall, features), jnp.bfloat16),
            pltpu.VMEM((LANES, tall), jnp.int32),
            pltpu.VMEM((views, 1, 2 * tall), jnp.float32),
            pltpu.VMEM((owners, 2, 1, 2 * half), jnp.float32),
            pltpu.VMEM((views, deep, width), jnp.bfloat16),
            pltpu.VMEM((views, deep, width), jnp.bfloat16),
            pltpu.VMEM((chips * pad, features), jnp.float32),
            pltpu.VMEM((chips * pad, features), jnp.float32),
            pltpu.VMEM((chips * pad, features), jnp.float32),
            pltpu.VMEM((chips, pad, features), jnp.bfloat16),
            pltpu.VMEM((chips, pad, features), jnp.bfloat16),
            dma((3,)),
            dma((chips,)),
            dma((2, chips)),
            dma((chips,)),
            dma((views,)),
            dma((views,)),
            dma((owners,)),
            dma((owners,)),
            dma((views,)),
            dma((views,)),
            dma,
            dma,
            dma((chips,)),
            dma((chips,)),
        ],
        compiler_params=pltpu.CompilerParams(
            collective_id=0, has_side_effects=True, vmem_limit_bytes=60 * 1024 * 1024
        ),
    )(first_view, second_view, partner.reshape(1, rows))


def solution(mesh):
    in_specs = (P("owner", None), P(("owner", "view"), None), P("owner"))
    out_specs = (P("owner", "view"), P(("owner", "view"), None))
    return jax.shard_map(shards, mesh=mesh, in_specs=in_specs, out_specs=out_specs, check_vma=False)
```

```python
import functools
import math

import jax
import jax.numpy as jnp
from jax import lax
from jax.experimental import pallas as pl
from jax.experimental.pallas import tpu as pltpu
from jax.sharding import PartitionSpec as P

LOW = -1e30
LANES = 128


def round_up(value, multiple):
    return (value + multiple - 1) // multiple * multiple


def kernel(
    owners, views, shard_rows,
    first_ref, second_ref, partner_ref, g1_ref, g2_ref,
    first_in, second_in, partner_in, xs, fz, pbuf, row_msg, col_msg, part1_send, part1_recv, merge_send, merge_recv, own2, part2_send, part2_recv,
    in_sem, x_send, x_recv, xf_send, row_send, row_recv, col_send, col_recv, p1_send, p1_recv, m_send, m_recv, p2_send, p2_recv,
):
    chips = owners // 2
    rows, features = first_ref.shape
    pad = xs.shape[2]
    half = chips * pad
    tall = fz.shape[0]
    width = features // views
    scale = 2.0 / math.sqrt(features)
    owner = lax.axis_index("owner")
    view = lax.axis_index("view")
    chip = owner // 2
    core = owner % 2
    other = 1 - core

    def send(src, dst, send_sem, recv_sem, to_owner, to_view):
        return pltpu.make_async_remote_copy(
            src_ref=src, dst_ref=dst, send_sem=send_sem, recv_sem=recv_sem,
            device_id=(to_owner, to_view), device_id_type=pl.DeviceIdType.MESH,
        )

    loads = [
        pltpu.make_async_copy(src, dst, in_sem.at[k])
        for k, (src, dst) in enumerate([(second_ref, second_in), (first_ref, first_in), (partner_ref, partner_in)])
    ]
    barrier = pltpu.get_barrier_semaphore()
    for k in range(1, owners):
        pl.semaphore_signal(
            barrier, inc=1, device_id=((owner + k) % owners, view), device_id_type=pl.DeviceIdType.MESH
        )
    for k in range(1, views):
        pl.semaphore_signal(
            barrier, inc=1, device_id=(owner, (view + k) % views), device_id_type=pl.DeviceIdType.MESH
        )
    for load in loads:
        load.start()
    loads[0].wait()
    mine = second_in[...]
    xs[core, chip] = jnp.concatenate([mine, jnp.zeros((pad - shard_rows, features), mine.dtype)], axis=0)
    pl.semaphore_wait(barrier, owners - 1 + views - 1)

    waits = []

    def block_send(core_of, chip_of, sems, index, to_owner):
        block = xs.at[core_of, chip_of]
        copy = send(block, block, sems.at[index], x_recv.at[core_of, chip_of], to_owner, view)
        copy.start()
        waits.append(copy)

    for k in range(1, chips):
        block_send(core, chip, x_send, k, (chip + k) % chips * 2 + core)
    block_send(core, chip, x_send, 0, chip * 2 + other)

    loads[1].wait()
    loads[2].wait()
    fz[0:rows, :] = first_in[...]
    fz[rows:tall, :] = jnp.zeros((tall - rows, features), fz.dtype)
    pbuf[...] = jnp.zeros_like(pbuf)
    pbuf[:, 0:rows] = jnp.broadcast_to(partner_in[...], (LANES, rows))
    copies = round_up(half, LANES) // LANES

    def spread(column):
        return jnp.concatenate([column] * copies, axis=1)[:, 0:half]

    partner = spread(pbuf[...].T[0:rows])
    position = lax.broadcasted_iota(jnp.int32, (1, half), 1)
    inner = position % pad
    slot = position // pad
    valid = inner < shard_rows

    def target_of(core_of):
        ids = ((slot * 2 + core_of) * views + view) * shard_rows + inner
        return (partner == jnp.where(valid, ids, -1)).astype(jnp.float32)

    sides = (core, other)
    targets = [target_of(side) for side in sides]

    def block_wait(core_of, chip_of):
        block = xs.at[core_of, chip_of]
        send(block, block, x_send.at[0], x_recv.at[core_of, chip_of], owner, view).wait_recv()

    def score(side):
        block = xs[side].reshape(half, features)
        values = scale * lax.dot_general(
            first_in[...], block, (((1,), (1,)), ((), ())), preferred_element_type=jnp.float32
        )
        return jnp.where(valid, values, LOW)

    def col_stats(side, values):
        peak = jnp.max(values, axis=0, keepdims=True)
        col_msg[owner, side, :, 0:half] = peak
        col_msg[owner, side, :, half:] = jnp.sum(jnp.exp(values - peak), axis=0, keepdims=True)

    def row_stats(values):
        peak = jnp.max(values, axis=1, keepdims=True)
        return [peak, jnp.sum(jnp.exp(values - peak), axis=1, keepdims=True)]

    for k in range(1, chips):
        source = (chip + chips - k) % chips
        block_wait(core, source)
        block_send(core, source, xf_send, k, chip * 2 + other)
    scores = [score(core)]
    col_stats(core, scores[0])
    row_parts = row_stats(scores[0])
    for k in range(chips):
        block_wait(other, (chip + chips - k) % chips)
    scores.append(score(other))
    col_stats(other, scores[1])
    for k in range(1, owners):
        to = (owner + k) % owners
        copy = send(col_msg.at[owner], col_msg.at[owner], col_send.at[k], col_recv.at[owner], to, view)
        copy.start()
        waits.append(copy)
    row_parts += row_stats(scores[1])
    lane = lax.broadcasted_iota(jnp.int32, (rows, LANES), 1)
    stats = row_parts[3]
    for k in (2, 1, 0):
        stats = jnp.where(lane == k, row_parts[k], stats)
    stats = jnp.concatenate([stats, jnp.zeros((tall - rows, LANES), jnp.float32)], axis=0).T
    peak = jnp.maximum(stats[0:1], stats[2:3])
    row_msg[view, :, 0:tall] = peak
    row_msg[view, :, tall:] = stats[1:2] * jnp.exp(stats[0:1] - peak) + stats[3:4] * jnp.exp(stats[2:3] - peak)
    for k in range(1, views):
        to = (view + k) % views
        copy = send(row_msg.at[view], row_msg.at[view], row_send.at[k], row_recv.at[view], owner, to)
        copy.start()
        waits.append(copy)
    for k in range(1, owners):
        source = (owner + k) % owners
        send(col_msg.at[source], col_msg.at[source], col_send.at[0], col_recv.at[source], owner, view).wait_recv()

    def log_sum(parts, length):
        peaks = [part[:, 0:length] for part in parts]
        peak = functools.reduce(jnp.maximum, peaks)
        mass = sum(part[:, length:] * jnp.exp(own - peak) for part, own in zip(parts, peaks))
        return peak + jnp.log(mass)

    by_col = [
        jnp.exp(values - log_sum([col_msg[k, side] for k in range(owners)], half))
        for side, values in zip(sides, scores)
    ]
    for k in range(1, views):
        source = (view + k) % views
        send(row_msg.at[source], row_msg.at[source], row_send.at[0], row_recv.at[source], owner, view).wait_recv()
    row_lse = log_sum([row_msg[k] for k in range(views)], tall)
    row_lse = spread(jnp.broadcast_to(row_lse, (LANES, tall)).T[0:rows])
    weights = [
        0.5 * (jnp.exp(values - row_lse) + by) - target for values, by, target in zip(scores, by_col, targets)
    ]

    left = [values.astype(jnp.bfloat16) for values in weights]

    def part1(index):
        start = pl.multiple_of(index * width, LANES)
        return scale * sum(
            jnp.dot(
                values, xs[side, :, :, pl.ds(start, width)].reshape(half, width),
                preferred_element_type=jnp.float32,
            )
            for side, values in zip(sides, left)
        )

    side = view // 2
    parity = view % 2
    is_end = side == parity
    far, middle, mate = 3 * (1 - side), 2 - side, view + 1 - 2 * parity

    def part1_copy(step, slot, to):
        return send(part1_send.at[step], part1_recv.at[slot], p1_send.at[step], p1_recv.at[slot], owner, to)

    def part1_start(step, slot, to):
        copy = part1_copy(step, slot, to)
        copy.start()
        waits.append(copy)

    def part1_wait(slot):
        part1_copy(0, slot, mate).wait_recv()
        return part1_recv[slot, 0:rows].astype(jnp.float32)

    def pick(at_end, at_middle):
        return jnp.where(is_end, at_end, at_middle)

    part1_send[0, 0:rows] = part1(pick(far, middle)).astype(jnp.bfloat16)
    part1_start(0, pick(0, 1 + parity), pick(mate, middle))
    part1_send[1, 0:rows] = part1(pick(middle, mate)).astype(jnp.bfloat16)
    part1_start(1, pick(1 + parity, 3), pick(middle, mate))

    def part2(values):
        tall_values = jnp.concatenate([values, jnp.zeros((tall - rows, half), jnp.float32)], axis=0)
        product = scale * jnp.dot(tall_values.T.astype(jnp.bfloat16), fz[...], preferred_element_type=jnp.float32)
        return product.reshape(chips, pad, features)

    merge_send[...] = part2(weights[1])

    def merge_copy(index):
        return send(
            merge_send.at[index], merge_recv.at[index], m_send.at[index], m_recv.at[index], chip * 2 + other, view
        )

    order = [(chip + k) % chips for k in list(range(1, chips)) + [0]]
    for index in order:
        copy = merge_copy(index)
        copy.start()
        waits.append(copy)
    own2[...] = part2(weights[0])
    last1 = part1(pick(mate, far))

    @pl.when(is_end)
    def _():
        part1_send[2, 0:rows] = last1.astype(jnp.bfloat16)
        part1_copy(2, 3, mate).start()

    own1 = part1(view)

    def merged(index):
        merge_copy(index).wait_recv()
        return own2[index] + merge_recv[index]

    for k in range(1, chips):
        to = order[k - 1]
        part2_send[k] = merged(to).astype(jnp.bfloat16)
        copy = send(part2_send.at[k], part2_recv.at[k], p2_send.at[k], p2_recv.at[k], to * 2 + core, view)
        copy.start()
        waits.append(copy)

    @pl.when(jnp.logical_not(is_end))
    def _():
        part1_send[2, 0:rows] = (last1 + part1_wait(0)).astype(jnp.bfloat16)
        part1_copy(2, 0, far).start()

    waits.append(part1_copy(2, 0, far))
    total2 = merged(chip)
    for k in range(1, chips):
        send(part2_send.at[k], part2_recv.at[k], p2_send.at[k], p2_recv.at[k], owner, view).wait_recv()
        total2 += part2_recv[k].astype(jnp.float32)
    g2_ref[...] = total2[0:shard_rows]
    own1 += part1_wait(3)

    @pl.when(is_end)
    def _():
        g1_ref[...] = own1 + part1_wait(0)

    @pl.when(jnp.logical_not(is_end))
    def _():
        g1_ref[...] = own1 + part1_wait(1) + part1_wait(2)

    for copy in waits:
        copy.wait_send()


def shards(first_view, second_view, partner):
    owners = lax.axis_size("owner")
    views = lax.axis_size("view")
    chips = owners // 2
    rows, features = first_view.shape
    shard_rows = second_view.shape[0]
    pad = round_up(shard_rows, 16)
    half = chips * pad
    tall = round_up(rows, LANES)
    deep = round_up(rows, 16)
    width = features // views
    dma = pltpu.SemaphoreType.DMA
    vmem = pl.BlockSpec(memory_space=pltpu.VMEM)
    hbm = pl.BlockSpec(memory_space=pl.ANY)
    return pl.pallas_call(
        functools.partial(kernel, owners, views, shard_rows),
        out_shape=(
            pltpu.VMEM((rows, width), jnp.float32),
            pltpu.VMEM((shard_rows, features), jnp.float32),
        ),
        in_specs=[hbm] * 3,
        out_specs=(vmem, vmem),
        scratch_shapes=[
            pltpu.VMEM((rows, features), jnp.bfloat16),
            pltpu.VMEM((shard_rows, features), jnp.bfloat16),
            pltpu.VMEM((1, rows), jnp.int32),
            pltpu.VMEM((2, chips, pad, features), jnp.bfloat16),
            pltpu.VMEM((tall, features), jnp.bfloat16),
            pltpu.VMEM((LANES, tall), jnp.int32),
            pltpu.VMEM((views, 1, 2 * tall), jnp.float32),
            pltpu.VMEM((owners, 2, 1, 2 * half), jnp.float32),
            pltpu.VMEM((views, deep, width), jnp.bfloat16),
            pltpu.VMEM((views, deep, width), jnp.bfloat16),
            pltpu.VMEM((chips, pad, features), jnp.float32),
            pltpu.VMEM((chips, pad, features), jnp.float32),
            pltpu.VMEM((chips, pad, features), jnp.float32),
            pltpu.VMEM((chips, pad, features), jnp.bfloat16),
            pltpu.VMEM((chips, pad, features), jnp.bfloat16),
            dma((3,)),
            dma((chips,)),
            dma((2, chips)),
            dma((chips,)),
            dma((views,)),
            dma((views,)),
            dma((owners,)),
            dma((owners,)),
            dma((views,)),
            dma((views,)),
            dma((chips,)),
            dma((chips,)),
            dma((chips,)),
            dma((chips,)),
        ],
        compiler_params=pltpu.CompilerParams(
            collective_id=0, has_side_effects=True, vmem_limit_bytes=60 * 1024 * 1024
        ),
    )(first_view, second_view, partner.reshape(1, rows))


def solution(mesh):
    in_specs = (P("owner", None), P(("owner", "view"), None), P("owner"))
    out_specs = (P("owner", "view"), P(("owner", "view"), None))
    return jax.shard_map(shards, mesh=mesh, in_specs=in_specs, out_specs=out_specs, check_vma=False)
```

```python
import functools
import math

import jax
import jax.numpy as jnp
from jax import lax
from jax.experimental import pallas as pl
from jax.experimental.pallas import tpu as pltpu
from jax.sharding import PartitionSpec as P

LOW = -1e30
LANES = 128


def round_up(value, multiple):
    return (value + multiple - 1) // multiple * multiple


def kernel(
    owners, views, shard_rows,
    first_ref, second_ref, partner_ref, g1_ref, g2_ref,
    first_in, second_in, partner_in, xs, fz, pbuf, row_msg, col_msg, part1_send, part1_recv, merge_send, merge_recv, own2, part2_send, part2_recv,
    in_sem, x_send, x_recv, xf_send, row_send, row_recv, col_send, col_recv, p1_send, p1_recv, relay_send, relay_recv, m_send, m_recv, p2_send, p2_recv,
):
    chips = owners // 2
    rows, features = first_ref.shape
    pad = xs.shape[2]
    half = chips * pad
    tall = fz.shape[0]
    width = features // views
    scale = 2.0 / math.sqrt(features)
    owner = lax.axis_index("owner")
    view = lax.axis_index("view")
    chip = owner // 2
    core = owner % 2
    other = 1 - core

    def send(src, dst, send_sem, recv_sem, to_owner, to_view):
        return pltpu.make_async_remote_copy(
            src_ref=src, dst_ref=dst, send_sem=send_sem, recv_sem=recv_sem,
            device_id=(to_owner, to_view), device_id_type=pl.DeviceIdType.MESH,
        )

    loads = [
        pltpu.make_async_copy(src, dst, in_sem.at[k])
        for k, (src, dst) in enumerate([(second_ref, second_in), (first_ref, first_in), (partner_ref, partner_in)])
    ]
    barrier = pltpu.get_barrier_semaphore()
    for k in range(1, owners):
        pl.semaphore_signal(
            barrier, inc=1, device_id=((owner + k) % owners, view), device_id_type=pl.DeviceIdType.MESH
        )
    for k in range(1, views):
        pl.semaphore_signal(
            barrier, inc=1, device_id=(owner, (view + k) % views), device_id_type=pl.DeviceIdType.MESH
        )
    for load in loads:
        load.start()
    loads[0].wait()
    mine = second_in[...]
    xs[core, chip] = jnp.concatenate([mine, jnp.zeros((pad - shard_rows, features), mine.dtype)], axis=0)
    pl.semaphore_wait(barrier, owners - 1 + views - 1)

    waits = []

    def block_send(core_of, chip_of, sems, index, to_owner):
        block = xs.at[core_of, chip_of]
        copy = send(block, block, sems.at[index], x_recv.at[core_of, chip_of], to_owner, view)
        copy.start()
        waits.append(copy)

    if chips == 4:
        peers = [3 - chip, (chip + 2) % 4, chip + 1 - 2 * (chip % 2)]
        sources = peers[::-1]
    else:
        peers = [(chip + k) % chips for k in range(1, chips)]
        sources = [(chip + chips - k) % chips for k in range(1, chips)]
    for k in range(1, chips):
        block_send(core, chip, x_send, k, peers[k - 1] * 2 + core)
    block_send(core, chip, x_send, 0, chip * 2 + other)

    loads[1].wait()
    loads[2].wait()
    fz[0:rows, :] = first_in[...]
    fz[rows:tall, :] = jnp.zeros((tall - rows, features), fz.dtype)
    pbuf[...] = jnp.zeros_like(pbuf)
    pbuf[:, 0:rows] = jnp.broadcast_to(partner_in[...], (LANES, rows))
    copies = round_up(half, LANES) // LANES

    def spread(column):
        return jnp.concatenate([column] * copies, axis=1)[:, 0:half]

    partner = spread(pbuf[...].T[0:rows])
    position = lax.broadcasted_iota(jnp.int32, (1, half), 1)
    inner = position % pad
    slot = position // pad
    valid = inner < shard_rows

    def target_of(core_of):
        ids = ((slot * 2 + core_of) * views + view) * shard_rows + inner
        return (partner == jnp.where(valid, ids, -1)).astype(jnp.float32)

    sides = (core, other)
    targets = [target_of(side) for side in sides]

    def block_wait(core_of, chip_of):
        block = xs.at[core_of, chip_of]
        send(block, block, x_send.at[0], x_recv.at[core_of, chip_of], owner, view).wait_recv()

    def score(side):
        block = xs[side].reshape(half, features)
        values = scale * lax.dot_general(
            first_in[...], block, (((1,), (1,)), ((), ())), preferred_element_type=jnp.float32
        )
        return jnp.where(valid, values, LOW)

    def col_stats(side, values):
        peak = jnp.max(values, axis=0, keepdims=True)
        col_msg[owner, side, :, 0:half] = peak
        col_msg[owner, side, :, half:] = jnp.sum(jnp.exp(values - peak), axis=0, keepdims=True)

    def row_stats(values):
        peak = jnp.max(values, axis=1, keepdims=True)
        return [peak, jnp.sum(jnp.exp(values - peak), axis=1, keepdims=True)]

    for k, source in enumerate(sources, 1):
        block_wait(core, source)
        block_send(core, source, xf_send, k, chip * 2 + other)
    scores = [score(core)]
    col_stats(core, scores[0])
    row_parts = row_stats(scores[0])
    for source in [chip] + sources:
        block_wait(other, source)
    scores.append(score(other))
    col_stats(other, scores[1])
    for k in range(1, owners):
        to = (owner + k) % owners
        copy = send(col_msg.at[owner], col_msg.at[owner], col_send.at[k], col_recv.at[owner], to, view)
        copy.start()
        waits.append(copy)
    row_parts += row_stats(scores[1])
    lane = lax.broadcasted_iota(jnp.int32, (rows, LANES), 1)
    stats = row_parts[3]
    for k in (2, 1, 0):
        stats = jnp.where(lane == k, row_parts[k], stats)
    stats = jnp.concatenate([stats, jnp.zeros((tall - rows, LANES), jnp.float32)], axis=0).T
    peak = jnp.maximum(stats[0:1], stats[2:3])
    row_msg[view, :, 0:tall] = peak
    row_msg[view, :, tall:] = stats[1:2] * jnp.exp(stats[0:1] - peak) + stats[3:4] * jnp.exp(stats[2:3] - peak)
    for k in range(1, views):
        to = (view + k) % views
        copy = send(row_msg.at[view], row_msg.at[view], row_send.at[k], row_recv.at[view], owner, to)
        copy.start()
        waits.append(copy)
    for k in range(1, owners):
        source = (owner + k) % owners
        send(col_msg.at[source], col_msg.at[source], col_send.at[0], col_recv.at[source], owner, view).wait_recv()

    def log_sum(parts, length):
        peaks = [part[:, 0:length] for part in parts]
        peak = functools.reduce(jnp.maximum, peaks)
        mass = sum(part[:, length:] * jnp.exp(own - peak) for part, own in zip(parts, peaks))
        return peak + jnp.log(mass)

    by_col = [
        jnp.exp(values - log_sum([col_msg[k, side] for k in range(owners)], half))
        for side, values in zip(sides, scores)
    ]
    for k in range(1, views):
        source = (view + k) % views
        send(row_msg.at[source], row_msg.at[source], row_send.at[0], row_recv.at[source], owner, view).wait_recv()
    row_lse = log_sum([row_msg[k] for k in range(views)], tall)
    row_lse = spread(jnp.broadcast_to(row_lse, (LANES, tall)).T[0:rows])
    weights = [
        0.5 * (jnp.exp(values - row_lse) + by) - target for values, by, target in zip(scores, by_col, targets)
    ]

    left = [values.astype(jnp.bfloat16) for values in weights]

    def part1(index):
        start = pl.multiple_of(index * width, LANES)
        return scale * sum(
            jnp.dot(
                values, xs[side, :, :, pl.ds(start, width)].reshape(half, width),
                preferred_element_type=jnp.float32,
            )
            for side, values in zip(sides, left)
        )

    side = view // 2
    parity = view % 2
    is_end = side == parity
    far, middle, mate = 3 * (1 - side), 2 - side, view + 1 - 2 * parity

    part = part1_send.shape[1] // 2
    spans = [(0, part), (part, rows)]

    def part1_copy(step, slot, to):
        return send(part1_send.at[step], part1_recv.at[slot], p1_send.at[step], p1_recv.at[slot], owner, to)

    def relay_copy(piece, to):
        span = pl.ds(piece * part, part)
        return send(
            part1_send.at[2, span], part1_recv.at[0, span], relay_send.at[piece], relay_recv.at[piece], owner, to
        )

    def part1_wait(slot):
        part1_copy(0, slot, mate).wait_recv()
        return part1_recv[slot, 0:rows].astype(jnp.float32)

    def relay_wait(piece):
        relay_copy(piece, mate).wait_recv()
        low, high = spans[piece]
        return part1_recv[0, low:high].astype(jnp.float32)

    def pick(at_end, at_middle):
        return jnp.where(is_end, at_end, at_middle)

    def by_place(at_end, at_middle):
        pl.when(is_end)(at_end)
        pl.when(jnp.logical_not(is_end))(at_middle)

    def middle_start(values):
        part1_send[0, 0:rows] = values.astype(jnp.bfloat16)
        part1_copy(0, 1 + parity, middle).start()

    def mate_start(values):
        part1_send[1, 0:rows] = values.astype(jnp.bfloat16)
        part1_copy(1, 3, mate).start()

    def relay_start(values):
        part1_send[2, 0:rows] = values.astype(jnp.bfloat16)
        for piece in range(2):
            relay_copy(piece, mate).start()

    def far_start(values):
        for piece, (low, high) in enumerate(spans):
            part1_send[2, low:high] = (values[low:high] + relay_wait(piece)).astype(jnp.bfloat16)
            relay_copy(piece, far).start()

    values1 = part1(pick(far, middle))
    by_place(lambda: relay_start(values1), lambda: middle_start(values1))
    values2 = part1(pick(middle, mate))
    by_place(lambda: middle_start(values2), lambda: mate_start(values2))
    waits += [part1_copy(0, 1, middle), part1_copy(1, 3, mate)]

    def part2(values):
        tall_values = jnp.concatenate([values, jnp.zeros((tall - rows, half), jnp.float32)], axis=0)
        product = scale * jnp.dot(tall_values.T.astype(jnp.bfloat16), fz[...], preferred_element_type=jnp.float32)
        return product.reshape(chips, pad, features)

    merge_send[...] = part2(weights[1])

    def merge_copy(index):
        return send(
            merge_send.at[index], merge_recv.at[index], m_send.at[index], m_recv.at[index], chip * 2 + other, view
        )

    for index in peers + [chip]:
        copy = merge_copy(index)
        copy.start()
        waits.append(copy)
    own2[...] = part2(weights[0])
    last1 = part1(pick(mate, far))

    pl.when(is_end)(lambda: mate_start(last1))
    own1 = part1(view)

    def merged(index):
        merge_copy(index).wait_recv()
        return own2[index] + merge_recv[index]

    for k in range(1, chips):
        to = peers[k - 1]
        part2_send[k] = merged(to).astype(jnp.bfloat16)
        copy = send(part2_send.at[k], part2_recv.at[k], p2_send.at[k], p2_recv.at[k], to * 2 + core, view)
        copy.start()
        waits.append(copy)

    pl.when(jnp.logical_not(is_end))(lambda: far_start(last1))
    waits += [relay_copy(piece, far) for piece in range(2)]
    total2 = merged(chip)
    for k in range(1, chips):
        send(part2_send.at[k], part2_recv.at[k], p2_send.at[k], p2_recv.at[k], owner, view).wait_recv()
        total2 += part2_recv[k].astype(jnp.float32)
    g2_ref[...] = total2[0:shard_rows]
    own1 += part1_wait(3)

    @pl.when(is_end)
    def _():
        for piece, (low, high) in enumerate(spans):
            g1_ref[low:high] = own1[low:high] + relay_wait(piece)

    @pl.when(jnp.logical_not(is_end))
    def _():
        g1_ref[...] = own1 + part1_wait(1) + part1_wait(2)

    for copy in waits:
        copy.wait_send()


def shards(first_view, second_view, partner):
    owners = lax.axis_size("owner")
    views = lax.axis_size("view")
    chips = owners // 2
    rows, features = first_view.shape
    shard_rows = second_view.shape[0]
    pad = round_up(shard_rows, 16)
    half = chips * pad
    tall = round_up(rows, LANES)
    deep = round_up(rows, 16)
    width = features // views
    dma = pltpu.SemaphoreType.DMA
    vmem = pl.BlockSpec(memory_space=pltpu.VMEM)
    hbm = pl.BlockSpec(memory_space=pl.ANY)
    return pl.pallas_call(
        functools.partial(kernel, owners, views, shard_rows),
        out_shape=(
            pltpu.VMEM((rows, width), jnp.float32),
            pltpu.VMEM((shard_rows, features), jnp.float32),
        ),
        in_specs=[hbm] * 3,
        out_specs=(vmem, vmem),
        scratch_shapes=[
            pltpu.VMEM((rows, features), jnp.bfloat16),
            pltpu.VMEM((shard_rows, features), jnp.bfloat16),
            pltpu.VMEM((1, rows), jnp.int32),
            pltpu.VMEM((2, chips, pad, features), jnp.bfloat16),
            pltpu.VMEM((tall, features), jnp.bfloat16),
            pltpu.VMEM((LANES, tall), jnp.int32),
            pltpu.VMEM((views, 1, 2 * tall), jnp.float32),
            pltpu.VMEM((owners, 2, 1, 2 * half), jnp.float32),
            pltpu.VMEM((views, deep, width), jnp.bfloat16),
            pltpu.VMEM((views, deep, width), jnp.bfloat16),
            pltpu.VMEM((chips, pad, features), jnp.float32),
            pltpu.VMEM((chips, pad, features), jnp.float32),
            pltpu.VMEM((chips, pad, features), jnp.float32),
            pltpu.VMEM((chips, pad, features), jnp.bfloat16),
            pltpu.VMEM((chips, pad, features), jnp.bfloat16),
            dma((3,)),
            dma((chips,)),
            dma((2, chips)),
            dma((chips,)),
            dma((views,)),
            dma((views,)),
            dma((owners,)),
            dma((owners,)),
            dma((views,)),
            dma((views,)),
            dma((2,)),
            dma((2,)),
            dma((chips,)),
            dma((chips,)),
            dma((chips,)),
            dma((chips,)),
        ],
        compiler_params=pltpu.CompilerParams(
            collective_id=0, has_side_effects=True, vmem_limit_bytes=60 * 1024 * 1024
        ),
    )(first_view, second_view, partner.reshape(1, rows))


def solution(mesh):
    in_specs = (P("owner", None), P(("owner", "view"), None), P("owner"))
    out_specs = (P("owner", "view"), P(("owner", "view"), None))
    return jax.shard_map(shards, mesh=mesh, in_specs=in_specs, out_specs=out_specs, check_vma=False)
```

```python
import functools
import math

import jax
import jax.numpy as jnp
from jax import lax
from jax.experimental import pallas as pl
from jax.experimental.pallas import tpu as pltpu
from jax.sharding import PartitionSpec as P

LOW = -1e30
LANES = 128


def round_up(value, multiple):
    return (value + multiple - 1) // multiple * multiple


def kernel(
    owners, views, shard_rows,
    first_ref, second_ref, partner_ref, g1_ref, g2_ref,
    first_in, second_in, partner_in, xs, fz, pbuf, row_msg, col_msg, part1_send, part1_recv, merge_send, merge_recv, own2, part2_send, part2_recv,
    in_sem, x_send, x_recv, xf_send, row_send, row_recv, col_send, col_recv, p1_send, p1_recv, relay_send, relay_recv, m_send, m_recv, p2_send, p2_recv,
):
    chips = owners // 2
    rows, features = first_ref.shape
    pad = xs.shape[2]
    half = chips * pad
    tall = fz.shape[0]
    width = features // views
    scale = 2.0 / math.sqrt(features)
    owner = lax.axis_index("owner")
    view = lax.axis_index("view")
    chip = owner // 2
    core = owner % 2
    other = 1 - core

    def send(src, dst, send_sem, recv_sem, to_owner, to_view):
        return pltpu.make_async_remote_copy(
            src_ref=src, dst_ref=dst, send_sem=send_sem, recv_sem=recv_sem,
            device_id=(to_owner, to_view), device_id_type=pl.DeviceIdType.MESH,
        )

    loads = [
        pltpu.make_async_copy(src, dst, in_sem.at[k])
        for k, (src, dst) in enumerate([(second_ref, second_in), (first_ref, first_in), (partner_ref, partner_in)])
    ]
    for load in loads:
        load.start()
    barrier = pltpu.get_barrier_semaphore()
    for k in range(1, owners):
        pl.semaphore_signal(
            barrier, inc=1, device_id=((owner + k) % owners, view), device_id_type=pl.DeviceIdType.MESH
        )
    for k in range(1, views):
        pl.semaphore_signal(
            barrier, inc=1, device_id=(owner, (view + k) % views), device_id_type=pl.DeviceIdType.MESH
        )
    loads[0].wait()
    mine = second_in[...]
    xs[core, chip] = jnp.concatenate([mine, jnp.zeros((pad - shard_rows, features), mine.dtype)], axis=0)
    pl.semaphore_wait(barrier, owners - 1 + views - 1)

    waits = []

    def block_send(core_of, chip_of, sems, index, to_owner):
        block = xs.at[core_of, chip_of]
        copy = send(block, block, sems.at[index], x_recv.at[core_of, chip_of], to_owner, view)
        copy.start()
        waits.append(copy)

    if chips == 4:
        peers = [3 - chip, (chip + 2) % 4, chip + 1 - 2 * (chip % 2)]
        sources = peers[::-1]
    else:
        peers = [(chip + k) % chips for k in range(1, chips)]
        sources = [(chip + chips - k) % chips for k in range(1, chips)]
    for k in range(1, chips):
        block_send(core, chip, x_send, k, peers[k - 1] * 2 + core)
    block_send(core, chip, x_send, 0, chip * 2 + other)

    loads[1].wait()
    loads[2].wait()
    fz[0:rows, :] = first_in[...]
    fz[rows:tall, :] = jnp.zeros((tall - rows, features), fz.dtype)
    pbuf[...] = jnp.zeros_like(pbuf)
    pbuf[:, 0:rows] = jnp.broadcast_to(partner_in[...], (LANES, rows))
    copies = round_up(half, LANES) // LANES

    def spread(column):
        return jnp.concatenate([column] * copies, axis=1)[:, 0:half]

    partner = spread(pbuf[...].T[0:rows])
    position = lax.broadcasted_iota(jnp.int32, (1, half), 1)
    inner = position % pad
    slot = position // pad
    valid = inner < shard_rows

    def target_of(core_of):
        ids = ((slot * 2 + core_of) * views + view) * shard_rows + inner
        return (partner == jnp.where(valid, ids, -1)).astype(jnp.float32)

    sides = (core, other)
    targets = [target_of(side) for side in sides]

    def block_wait(core_of, chip_of):
        block = xs.at[core_of, chip_of]
        send(block, block, x_send.at[0], x_recv.at[core_of, chip_of], owner, view).wait_recv()

    def score(side):
        block = xs[side].reshape(half, features)
        values = scale * lax.dot_general(
            first_in[...], block, (((1,), (1,)), ((), ())), preferred_element_type=jnp.float32
        )
        return jnp.where(valid, values, LOW)

    def col_stats(side, values):
        peak = jnp.max(values, axis=0, keepdims=True)
        col_msg[owner, side, :, 0:half] = peak
        col_msg[owner, side, :, half:] = jnp.sum(jnp.exp(values - peak), axis=0, keepdims=True)

    def row_stats(values):
        peak = jnp.max(values, axis=1, keepdims=True)
        return [peak, jnp.sum(jnp.exp(values - peak), axis=1, keepdims=True)]

    for k, source in enumerate(sources, 1):
        block_wait(core, source)
        block_send(core, source, xf_send, k, chip * 2 + other)
    scores = [score(core)]
    col_stats(core, scores[0])
    row_parts = row_stats(scores[0])
    for source in [chip] + sources:
        block_wait(other, source)
    scores.append(score(other))
    col_stats(other, scores[1])
    for k in range(1, owners):
        to = (owner + k) % owners
        copy = send(col_msg.at[owner], col_msg.at[owner], col_send.at[k], col_recv.at[owner], to, view)
        copy.start()
        waits.append(copy)
    row_parts += row_stats(scores[1])
    lane = lax.broadcasted_iota(jnp.int32, (rows, LANES), 1)
    stats = row_parts[3]
    for k in (2, 1, 0):
        stats = jnp.where(lane == k, row_parts[k], stats)
    stats = jnp.concatenate([stats, jnp.zeros((tall - rows, LANES), jnp.float32)], axis=0).T
    peak = jnp.maximum(stats[0:1], stats[2:3])
    row_msg[view, :, 0:tall] = peak
    row_msg[view, :, tall:] = stats[1:2] * jnp.exp(stats[0:1] - peak) + stats[3:4] * jnp.exp(stats[2:3] - peak)
    for k in range(1, views):
        to = (view + k) % views
        copy = send(row_msg.at[view], row_msg.at[view], row_send.at[k], row_recv.at[view], owner, to)
        copy.start()
        waits.append(copy)
    for k in range(1, owners):
        source = (owner + k) % owners
        send(col_msg.at[source], col_msg.at[source], col_send.at[0], col_recv.at[source], owner, view).wait_recv()

    def log_sum(parts, length):
        peaks = [part[:, 0:length] for part in parts]
        peak = functools.reduce(jnp.maximum, peaks)
        mass = sum(part[:, length:] * jnp.exp(own - peak) for part, own in zip(parts, peaks))
        return peak + jnp.log(mass)

    by_col = [
        jnp.exp(values - log_sum([col_msg[k, side] for k in range(owners)], half))
        for side, values in zip(sides, scores)
    ]
    for k in range(1, views):
        source = (view + k) % views
        send(row_msg.at[source], row_msg.at[source], row_send.at[0], row_recv.at[source], owner, view).wait_recv()
    row_lse = log_sum([row_msg[k] for k in range(views)], tall)
    row_lse = spread(jnp.broadcast_to(row_lse, (LANES, tall)).T[0:rows])
    weights = [
        0.5 * (jnp.exp(values - row_lse) + by) - target for values, by, target in zip(scores, by_col, targets)
    ]

    left = [values.astype(jnp.bfloat16) for values in weights]

    def part1(index):
        start = pl.multiple_of(index * width, LANES)
        return scale * sum(
            jnp.dot(
                values, xs[side, :, :, pl.ds(start, width)].reshape(half, width),
                preferred_element_type=jnp.float32,
            )
            for side, values in zip(sides, left)
        )

    side = view // 2
    parity = view % 2
    is_end = side == parity
    far, middle, mate = 3 * (1 - side), 2 - side, view + 1 - 2 * parity

    part = part1_send.shape[1] // 2
    spans = [(0, part), (part, rows)]

    def part1_copy(step, slot, to):
        return send(part1_send.at[step], part1_recv.at[slot], p1_send.at[step], p1_recv.at[slot], owner, to)

    def relay_copy(piece, to):
        span = pl.ds(piece * part, part)
        return send(
            part1_send.at[2, span], part1_recv.at[0, span], relay_send.at[piece], relay_recv.at[piece], owner, to
        )

    def part1_wait(slot):
        part1_copy(0, slot, mate).wait_recv()
        return part1_recv[slot, 0:rows].astype(jnp.float32)

    def relay_wait(piece):
        relay_copy(piece, mate).wait_recv()
        low, high = spans[piece]
        return part1_recv[0, low:high].astype(jnp.float32)

    def pick(at_end, at_middle):
        return jnp.where(is_end, at_end, at_middle)

    def by_place(at_end, at_middle):
        pl.when(is_end)(at_end)
        pl.when(jnp.logical_not(is_end))(at_middle)

    def middle_start(values):
        part1_send[0, 0:rows] = values.astype(jnp.bfloat16)
        part1_copy(0, 1 + parity, middle).start()

    def mate_start(values):
        part1_send[1, 0:rows] = values.astype(jnp.bfloat16)
        part1_copy(1, 3, mate).start()

    def relay_start(values):
        part1_send[2, 0:rows] = values.astype(jnp.bfloat16)
        for piece in range(2):
            relay_copy(piece, mate).start()

    def far_start(values):
        for piece, (low, high) in enumerate(spans):
            part1_send[2, low:high] = (values[low:high] + relay_wait(piece)).astype(jnp.bfloat16)
            relay_copy(piece, far).start()

    values1 = part1(pick(far, middle))
    by_place(lambda: relay_start(values1), lambda: middle_start(values1))
    values2 = part1(pick(middle, mate))
    by_place(lambda: middle_start(values2), lambda: mate_start(values2))
    waits += [part1_copy(0, 1, middle), part1_copy(1, 3, mate)]

    def part2(values):
        tall_values = jnp.concatenate([values, jnp.zeros((tall - rows, half), jnp.float32)], axis=0)
        product = scale * jnp.dot(tall_values.T.astype(jnp.bfloat16), fz[...], preferred_element_type=jnp.float32)
        return product.reshape(chips, pad, features)

    merge_send[...] = part2(weights[1])

    def merge_copy(index):
        return send(
            merge_send.at[index], merge_recv.at[index], m_send.at[index], m_recv.at[index], chip * 2 + other, view
        )

    for index in peers + [chip]:
        copy = merge_copy(index)
        copy.start()
        waits.append(copy)
    own2[...] = part2(weights[0])
    last1 = part1(pick(mate, far))

    pl.when(is_end)(lambda: mate_start(last1))
    own1 = part1(view)

    def merged(index):
        merge_copy(index).wait_recv()
        return own2[index] + merge_recv[index]

    for k in range(1, chips):
        to = peers[k - 1]
        part2_send[k] = merged(to).astype(jnp.bfloat16)
        copy = send(part2_send.at[k], part2_recv.at[k], p2_send.at[k], p2_recv.at[k], to * 2 + core, view)
        copy.start()
        waits.append(copy)

    pl.when(jnp.logical_not(is_end))(lambda: far_start(last1))
    waits += [relay_copy(piece, far) for piece in range(2)]
    total2 = merged(chip)
    for k in range(1, chips):
        send(part2_send.at[k], part2_recv.at[k], p2_send.at[k], p2_recv.at[k], owner, view).wait_recv()
        total2 += part2_recv[k].astype(jnp.float32)
    g2_ref[...] = total2[0:shard_rows]
    own1 += part1_wait(3)

    @pl.when(is_end)
    def _():
        for piece, (low, high) in enumerate(spans):
            g1_ref[low:high] = own1[low:high] + relay_wait(piece)

    @pl.when(jnp.logical_not(is_end))
    def _():
        g1_ref[...] = own1 + part1_wait(1) + part1_wait(2)

    for copy in waits:
        copy.wait_send()


def shards(first_view, second_view, partner):
    owners = lax.axis_size("owner")
    views = lax.axis_size("view")
    chips = owners // 2
    rows, features = first_view.shape
    shard_rows = second_view.shape[0]
    pad = round_up(shard_rows, 16)
    half = chips * pad
    tall = round_up(rows, LANES)
    deep = round_up(rows, 16)
    width = features // views
    dma = pltpu.SemaphoreType.DMA
    vmem = pl.BlockSpec(memory_space=pltpu.VMEM)
    hbm = pl.BlockSpec(memory_space=pl.ANY)
    return pl.pallas_call(
        functools.partial(kernel, owners, views, shard_rows),
        out_shape=(
            pltpu.VMEM((rows, width), jnp.float32),
            pltpu.VMEM((shard_rows, features), jnp.float32),
        ),
        in_specs=[hbm] * 3,
        out_specs=(vmem, vmem),
        scratch_shapes=[
            pltpu.VMEM((rows, features), jnp.bfloat16),
            pltpu.VMEM((shard_rows, features), jnp.bfloat16),
            pltpu.VMEM((1, rows), jnp.int32),
            pltpu.VMEM((2, chips, pad, features), jnp.bfloat16),
            pltpu.VMEM((tall, features), jnp.bfloat16),
            pltpu.VMEM((LANES, tall), jnp.int32),
            pltpu.VMEM((views, 1, 2 * tall), jnp.float32),
            pltpu.VMEM((owners, 2, 1, 2 * half), jnp.float32),
            pltpu.VMEM((views, deep, width), jnp.bfloat16),
            pltpu.VMEM((views, deep, width), jnp.bfloat16),
            pltpu.VMEM((chips, pad, features), jnp.float32),
            pltpu.VMEM((chips, pad, features), jnp.float32),
            pltpu.VMEM((chips, pad, features), jnp.float32),
            pltpu.VMEM((chips, pad, features), jnp.bfloat16),
            pltpu.VMEM((chips, pad, features), jnp.bfloat16),
            dma((3,)),
            dma((chips,)),
            dma((2, chips)),
            dma((chips,)),
            dma((views,)),
            dma((views,)),
            dma((owners,)),
            dma((owners,)),
            dma((views,)),
            dma((views,)),
            dma((2,)),
            dma((2,)),
            dma((chips,)),
            dma((chips,)),
            dma((chips,)),
            dma((chips,)),
        ],
        compiler_params=pltpu.CompilerParams(
            collective_id=0, has_side_effects=True, vmem_limit_bytes=60 * 1024 * 1024
        ),
    )(first_view, second_view, partner.reshape(1, rows))


def solution(mesh):
    in_specs = (P("owner", None), P(("owner", "view"), None), P("owner"))
    out_specs = (P("owner", "view"), P(("owner", "view"), None))
    return jax.shard_map(shards, mesh=mesh, in_specs=in_specs, out_specs=out_specs, check_vma=False)
```
